32 devices in a mesh: grp: 2 (over x), seq: 16 (over z, y, core).
Axes of the slice: x: 2, y: 2, z: 4, core: 2. Of those that a mesh axis runs over, the one named last changes fastest.
Arguments:
- tokens: bfloat16 [16384, 1024], P(('grp', 'seq')), parts along dimension 0, may hold values from -6 to 6
- value_weight: bfloat16 [1024, 1024], replicated, may hold values from -0.1875 to 0.1875
- gate_weight: bfloat16 [1024, 1024], replicated, may hold values from -0.1875 to 0.1875
- out_weight: bfloat16 [1024, 1024], replicated, may hold values from -0.1875 to 0.1875
- kernel_weight: bfloat16 [1024, 16], replicated, may hold values from -0.1875 to 0.1875
- kernel_bias: float32 [16], replicated, may hold values from -4 to 4
Outputs:
- mixed: bfloat16 [16384, 1024], P(('grp', 'seq')), parts along dimension 0
The draws below stay inside these ranges and needn't reach their ends.
There are 2 independent parts, one for each index of `grp`. The reference program is written for one: setup_inputs(seed, part) draws one part's arguments, and reference() takes and returns one part's arrays. A program takes and returns all parts, laid end to end along the dimension named above; an argument that names none is the same for every part. Nothing has to cross between parts.
All inputs are finite; a program needn't handle non-finite values.
Results may differ from the reference program's by a relative error of at most 0.0071.
Values may be sent and summed in bfloat16 or wider, within the bound.
No kernel may reach another device: no remote copies, remote signals or barrier semaphores. Data moves between devices by JAX's collectives and lax.ppermute only.
A program may use at most 128 MiB of HBM per device.

```python
import jax
import jax.numpy as jnp

D = 1024
HEADS = 16
HS = 64
TOKENS = 8192


def block_levels(rng, extent, split, low, top_value):
    def one(position, blocks):
        steps = jax.random.uniform(jax.random.fold_in(jax.random.fold_in(rng, 6), position), (blocks,), jnp.float32, low / len(split), top_value / len(split))
        return jnp.repeat(jnp.exp(steps), extent[position] // blocks).reshape((-1,) + (1,) * (len(extent) - position - 1))

    factor_of = one(*split[0])
    for cut in split[1:]:
        factor_of = factor_of * one(*cut)
    return factor_of


def scatter_about(rng, dims, width, reach, split=(), dtype=jnp.bfloat16):
    level = block_levels(rng, dims, split, -0.22, 0.18) if split else 1.0
    array = jax.random.normal(rng, dims, jnp.float32) * width * level
    return jnp.minimum(jnp.maximum(array, -reach), reach).astype(dtype)


def setup_inputs(seed: int = 0, part: int = 0) -> dict:
    arg_keys = jax.random.split(jax.random.key(seed), 7)
    own_keys = jax.random.split(jax.random.fold_in(arg_keys[6], part), 7)
    tokens = scatter_about(own_keys[0], (TOKENS, D), 1.0, 6.0, ((0, 16),))
    value_weight = scatter_about(arg_keys[1], (D, D), D ** -0.5, 0.1875)
    gate_weight = scatter_about(arg_keys[2], (D, D), D ** -0.5, 0.1875)
    out_weight = scatter_about(arg_keys[3], (D, D), D ** -0.5, 0.1875)
    kernel_weight = scatter_about(arg_keys[4], (D, HEADS), D ** -0.5, 0.1875)
    kernel_bias = scatter_about(arg_keys[5], (HEADS,), 1.0, 4.0, (), jnp.float32)
    return dict(tokens=tokens, value_weight=value_weight, gate_weight=gate_weight, out_weight=out_weight, kernel_weight=kernel_weight, kernel_bias=kernel_bias)


def reference(tokens, value_weight, gate_weight, out_weight, kernel_weight, kernel_bias):
    values = jnp.dot(tokens, value_weight, preferred_element_type=jnp.float32).astype(jnp.bfloat16)
    gate = jnp.dot(tokens, gate_weight, preferred_element_type=jnp.float32)
    logits = jnp.dot(tokens, kernel_weight, preferred_element_type=jnp.float32) + kernel_bias
    kernel = (jnp.tanh(logits) * (TOKENS ** -0.5)).astype(jnp.bfloat16)
    kernel_freq = jnp.fft.rfft(kernel.astype(jnp.float32), axis=0)
    value_freq = jnp.fft.rfft(values.astype(jnp.float32), axis=0)
    product = value_freq.reshape(-1, HEADS, HS) * kernel_freq[:, :, None]
    conv = jnp.fft.irfft(product, n=TOKENS, axis=0).reshape(TOKENS, D).astype(jnp.bfloat16)
    gated = (conv.astype(jnp.float32) * jax.nn.silu(gate)).astype(jnp.bfloat16)
    return jnp.dot(gated, out_weight, preferred_element_type=jnp.float32).astype(jnp.bfloat16)
```

```python
import functools

import jax
import jax.numpy as jnp
from jax import lax
from jax.experimental import pallas as pl
from jax.experimental.pallas import tpu as pltpu
from jax.sharding import PartitionSpec as P

f32 = jnp.float32
bf16 = jnp.bfloat16
LANES = 128
VMEM = pl.BlockSpec(memory_space=pltpu.VMEM)


def params():
    return pltpu.CompilerParams(vmem_limit_bytes=48 * 2**20)


def cost(flops, nbytes):
    return pl.CostEstimate(flops=flops, bytes_accessed=nbytes, transcendentals=0)


def lag_body(length, tokens, weight, bias, out):
    logits = jnp.dot(tokens[...], weight[...], preferred_element_type=f32) + bias[...]
    out[...] = (jnp.tanh(logits) * length ** (-0.5)).T.astype(bf16)


def lag_rows(tokens, weight, bias, length):
    rows, width = tokens.shape
    heads = weight.shape[1]
    return pl.pallas_call(
        functools.partial(lag_body, length),
        out_shape=jax.ShapeDtypeStruct((heads, rows), bf16),
        in_specs=[VMEM] * 3,
        out_specs=VMEM,
        compiler_params=params(),
        name="lag_rows",
    )(tokens, weight, bias.reshape(1, heads))


def values_body(tokens, weight, out):
    part = jnp.dot(tokens[...], weight[...], preferred_element_type=f32)
    out[...] = part.T.astype(bf16).reshape(out.shape)


def values_blocks(tokens, weight, devices):
    rows, width = tokens.shape
    per = width // devices
    step = max(per, min(width, 256))
    count = step // per
    return pl.pallas_call(
        values_body,
        grid=(width // step,),
        out_shape=jax.ShapeDtypeStruct((devices, per, rows), bf16),
        in_specs=[
            pl.BlockSpec((rows, width), lambda i: (0, 0)),
            pl.BlockSpec((width, step), lambda i: (0, i)),
        ],
        out_specs=pl.BlockSpec((count, per, rows), lambda i: (i, 0, 0)),
        compiler_params=params(),
        name="values",
    )(tokens, weight)


def gate_body(tokens, weight, out):
    gate = jnp.dot(tokens[...], weight[...], preferred_element_type=f32)
    out[...] = gate * jax.nn.sigmoid(gate)


def gate_rows(tokens, weight):
    rows, width = tokens.shape
    step = min(width, 256)
    return pl.pallas_call(
        gate_body,
        grid=(width // step,),
        out_shape=jax.ShapeDtypeStruct((rows, width), f32),
        in_specs=[
            pl.BlockSpec((rows, width), lambda i: (0, 0)),
            pl.BlockSpec((width, step), lambda i: (0, i)),
        ],
        out_specs=pl.BlockSpec((rows, step), lambda i: (0, i)),
        compiler_params=params(),
        cost_estimate=cost(2 * rows * width * width, 4 * rows * width + 2 * width * width),
        name="gate",
    )(tokens, weight)


def conv_body(group, lag, values, out, strip, twice, acc):
    count, channels, span = values.shape
    length = lag.shape[1]
    lead = span - LANES
    row = lag[...].astype(f32)
    for piece in range(LANES // 16):
        turned = pltpu.roll(
            jnp.broadcast_to(row, (16, length)), 16 * piece, 1, stride=1, stride_axis=0
        ).astype(bf16)
        strip[16 * piece : 16 * piece + 16, lead:] = turned
        strip[16 * piece : 16 * piece + 16, :lead] = turned[:, length - lead :]
    twice[:count] = values[...]
    twice[count:] = values[...]
    acc[...] = jnp.zeros_like(acc)

    def step(at, carry):
        left, right = [], []
        for inner in range(group):
            lag_block = at * group + inner
            left.append(twice[pl.ds(count - lag_block, count)].reshape(count * channels, span))
            for part in range(span // LANES):
                first = pl.multiple_of(span * lag_block + lead - LANES * part, LANES)
                right.append(strip[:, pl.ds(first, span)])
        acc[...] += jnp.dot(
            jnp.concatenate(left, axis=1), jnp.concatenate(right, axis=0), preferred_element_type=f32
        )
        return carry

    lax.fori_loop(0, count // group, step, 0)
    out[...] = acc[...].reshape(out.shape).astype(bf16)


def convolve(lag, values):
    count, channels, span = values.shape
    length = count * span
    return pl.pallas_call(
        functools.partial(conv_body, 4),
        out_shape=jax.ShapeDtypeStruct(values.shape, bf16),
        in_specs=[VMEM] * 2,
        out_specs=VMEM,
        scratch_shapes=[
            pltpu.VMEM((LANES, length + span - LANES), bf16),
            pltpu.VMEM((2 * count, channels, span), bf16),
            pltpu.VMEM((count * channels, span), f32),
        ],
        compiler_params=params(),
        name="conv",
    )(lag, values)


def mix_body(conv, gate, weight, out):
    gated = (conv[...].T.astype(f32) * gate[...]).astype(bf16)
    out[...] = jnp.dot(gated, weight[...], preferred_element_type=f32).astype(bf16)


def mix(conv, gate, weight):
    rows, width = gate.shape
    return pl.pallas_call(
        mix_body,
        out_shape=jax.ShapeDtypeStruct((rows, weight.shape[1]), bf16),
        in_specs=[VMEM] * 3,
        out_specs=VMEM,
        compiler_params=params(),
        name="mix",
    )(conv, gate, weight)


def body(tokens, value_weight, gate_weight, out_weight, kernel_weight, kernel_bias):
    rows, width = tokens.shape
    heads = kernel_weight.shape[1]
    devices = lax.axis_size("seq")
    length = rows * devices
    lags = lag_rows(tokens, kernel_weight, kernel_bias, length)
    spread = jnp.repeat(lags, devices // heads, axis=0)
    lag = lax.all_to_all(spread, "seq", split_axis=0, concat_axis=1, tiled=True)
    values = values_blocks(tokens, value_weight, devices)
    columns = lax.all_to_all(values, "seq", split_axis=0, concat_axis=0, tiled=True)
    gate = gate_rows(tokens, gate_weight)
    convolved = convolve(lag, columns)
    returned = lax.all_to_all(convolved, "seq", split_axis=0, concat_axis=0, tiled=True)
    return mix(returned.reshape(width, rows), gate, out_weight)


def solution(mesh):
    placed = (P(("grp", "seq"), None), P(), P(), P(), P(), P())
    return jax.shard_map(
        body, mesh=mesh, in_specs=placed, out_specs=P(("grp", "seq"), None), check_vma=False
    )
```

```python
import functools

import jax
import jax.numpy as jnp
from jax import lax
from jax.experimental import pallas as pl
from jax.experimental.pallas import tpu as pltpu
from jax.sharding import PartitionSpec as P

f32 = jnp.float32
bf16 = jnp.bfloat16
LANES = 128
TILE = 16
VMEM = pl.BlockSpec(memory_space=pltpu.VMEM)
PARAMS = pltpu.CompilerParams(vmem_limit_bytes=48 * 2**20)
LARGE = pltpu.CompilerParams(vmem_limit_bytes=62 * 2**20)


def cost(flops, nbytes):
    return pl.CostEstimate(flops=int(flops), bytes_accessed=int(nbytes), transcendentals=0)


def whole_block(shape):
    return pl.BlockSpec(shape, lambda i: (0,) * len(shape))


def shape_of(shape, dtype=bf16):
    return jax.ShapeDtypeStruct(shape, dtype)


def place():
    me = lax.axis_index("seq")
    return me // 2, lax.rem(me, 2)


def project_body(sizes, tokens, weight, lag_weight, lag_bias, *refs):
    devices, per, first, heads, rows = sizes
    out, lag_rows = refs[0], refs[-1]
    at = pl.program_id(0)
    count = weight.shape[1] // per
    tiles = rows // LANES

    @pl.when(at == 0)
    def _():
        logits = lax.dot_general(
            lag_weight[...], tokens[...], (((1,), (1,)), ((), ())), preferred_element_type=f32
        ) + lag_bias[...]
        lag_rows[...] = jnp.tanh(logits) * (rows * devices) ** (-0.5)

    part = jnp.dot(tokens[...], weight[...], preferred_element_type=f32).astype(bf16).T
    for group in range(count):
        block = part[per * group : per * group + first]
        for tile in range(tiles):
            out[group, first * tile : first * tile + first] = block[:, LANES * tile : LANES * tile + LANES]
        head = (at * count + group) * heads // devices
        row = lag_rows[pl.ds(head, 1), :]
        pieces = [row[:, LANES * tile : LANES * tile + LANES] for tile in range(tiles)]
        pieces.append(jnp.zeros((out.shape[1] - first * tiles - tiles, LANES), f32))
        out[group, first * tiles :] = jnp.concatenate(pieces, axis=0).astype(bf16)
    if first < per:
        keep, other = refs[1:3]
        chip, core = place()
        for pair in range(count // 2):
            low = part[per * 2 * pair + first : per * (2 * pair + 1)]
            high = part[per * (2 * pair + 1) + first : per * (2 * pair + 2)]
            slot = jnp.bitwise_xor(chip, at * (count // 2) + pair)
            keep[slot] = jnp.where(core == 0, low, high)
            other[slot] = jnp.where(core == 0, high, low)


def project(tokens, weight, lag_weight, lag_bias, devices, first):
    rows, width = tokens.shape
    heads = lag_weight.shape[1]
    per = width // devices
    step = max(2 * per, min(width, 256))
    count = step // per
    tall = first * (rows // LANES) + TILE
    outs = [shape_of((devices, tall, LANES))]
    specs = [pl.BlockSpec((count, tall, LANES), lambda i: (i, 0, 0))]
    if first < per:
        rest = (devices // 2, per - first, rows)
        outs += [shape_of(rest)] * 2
        specs += [whole_block(rest)] * 2
    return pl.pallas_call(
        functools.partial(project_body, (devices, per, first, heads, rows)),
        grid=(width // step,),
        out_shape=outs,
        in_specs=[
            whole_block((rows, width)),
            pl.BlockSpec((width, step), lambda i: (0, i)),
            whole_block((heads, width)),
            whole_block((heads, 1)),
        ],
        out_specs=specs,
        scratch_shapes=[pltpu.VMEM((heads, rows), f32)],
        compiler_params=LARGE,
        cost_estimate=cost(2 * rows * width * width, 4 * rows * width + 2 * width * width),
        name="project",
    )(tokens, weight, lag_weight.T, lag_bias.reshape(heads, 1))


def gate_body(tokens, weight, *refs):
    gate = jnp.dot(tokens[...], weight[...], preferred_element_type=f32)
    if len(refs) == 1:
        refs[0][...] = (gate / (1.0 + jnp.exp(-gate))).T
        return
    keep, other, out, *messages = refs
    out[...] = (gate / (1.0 + jnp.exp(-gate))).T

    @pl.when(pl.program_id(0) == 0)
    def _():
        for slot, message in enumerate(messages):
            message[0] = keep[slot]
            message[1] = other[slot]


def gate_columns(tokens, weight, pair):
    rows, width = tokens.shape
    step = min(width, 256)
    outs, out_specs, ins = [shape_of((width, rows), f32)], [pl.BlockSpec((step, rows), lambda i: (i, 0))], []
    if pair:
        chips, channels, _ = pair[0].shape
        outs += [shape_of((2, channels, rows))] * chips
        out_specs += [whole_block((2, channels, rows))] * chips
        ins = [whole_block(pair[0].shape)] * 2
    return pl.pallas_call(
        gate_body,
        grid=(width // step,),
        out_shape=outs,
        in_specs=[whole_block((rows, width)), pl.BlockSpec((width, step), lambda i: (0, i))] + ins,
        out_specs=out_specs,
        compiler_params=PARAMS,
        cost_estimate=cost(2 * rows * width * width, 4 * rows * width + 2 * width * width),
        name="gate",
    )(tokens, weight, *pair)


def fill_strips(row, plus, minus):
    length = row.shape[1]
    half = length // 2
    lead = plus.shape[1] - half
    low, high = row[:, :half] * 0.5, row[:, half:] * 0.5
    for ref, line, sign in ((plus, low + high, 1.0), (minus, low - high, -1.0)):
        for piece in range(LANES // TILE):
            turned = pltpu.roll(
                jnp.broadcast_to(line, (TILE, half)), TILE * piece, 1, stride=1, stride_axis=0
            )
            here = slice(TILE * piece, TILE * piece + TILE)
            edge = turned[:, :LANES]
            if sign < 0:
                down = lax.broadcasted_iota(jnp.int32, (TILE, LANES), 0) + TILE * piece
                across = lax.broadcasted_iota(jnp.int32, (TILE, LANES), 1)
                edge = jnp.where(across < down, -edge, edge)
            ref[here, :lead] = (turned[:, half - lead :] * sign).astype(bf16)
            ref[here, lead : lead + LANES] = edge.astype(bf16)
            ref[here, lead + LANES :] = turned[:, LANES:].astype(bf16)


def convolve(block_of, plus, minus, twice_plus, twice_minus, acc_plus, acc_minus):
    count, channels, span = twice_plus.shape
    half = count // 2
    lead = plus.shape[1] - half * span
    for at in range(half):
        low, high = block_of(at).astype(f32), block_of(at + half).astype(f32)
        total, gap = (low + high).astype(bf16), (low - high).astype(bf16)
        twice_plus[at] = total
        twice_plus[at + half] = total
        twice_minus[at] = -gap
        twice_minus[at + half] = gap
    group = min(half, 4)
    for acc, twice, strip in ((acc_plus, twice_plus, plus), (acc_minus, twice_minus, minus)):
        for start in range(0, half, group):
            left, right = [], []
            for lag in range(start, start + group):
                left.append(twice[half - lag : 2 * half - lag].reshape(half * channels, span))
                for part in range(span // LANES):
                    begin = span * lag + lead - LANES * part
                    right.append(strip[:, begin : begin + span])
            piece = jnp.dot(
                jnp.concatenate(left, axis=1), jnp.concatenate(right, axis=0), preferred_element_type=f32
            )
            acc[...] = piece if start == 0 else acc[...] + piece


def first_body(channels, values, *refs):
    out, plus, minus, *scratch = refs[-7:]
    count, tall, _ = values.shape
    span = out.shape[2]
    tiles = span // LANES
    pieces = []
    for at in range(count):
        rows = values[at, channels * tiles :].astype(f32)
        pieces += [rows[tile : tile + 1] for tile in range(tiles)]
    fill_strips(jnp.concatenate(pieces, axis=1), plus, minus)

    def block_of(at):
        return jnp.concatenate(
            [values[at, channels * tile : channels * tile + channels] for tile in range(tiles)], axis=1
        )

    convolve(block_of, plus, minus, *scratch)
    acc_plus, acc_minus = scratch[2:]
    half = count // 2
    out[:half] = (acc_plus[...] + acc_minus[...]).reshape(half, channels, span).astype(bf16)
    out[half:] = (acc_plus[...] - acc_minus[...]).reshape(half, channels, span).astype(bf16)


def scratch_for(count, channels, span):
    return [pltpu.VMEM((count, channels, span), bf16)] * 2 + [
        pltpu.VMEM((count // 2 * channels, span), f32)
    ] * 2


def convolve_first(values, channels, span, before):
    count = values.shape[0]
    strip = shape_of((LANES, count // 2 * span + span - LANES))
    return pl.pallas_call(
        functools.partial(first_body, channels),
        out_shape=[shape_of((count, channels, span)), strip, strip],
        in_specs=[VMEM] + [pl.BlockSpec(memory_space=pl.ANY)] * len(before),
        out_specs=[VMEM] * 3,
        scratch_shapes=scratch_for(count, channels, span),
        compiler_params=PARAMS,
        cost_estimate=cost(1e6, 1e5),
        name="conv_first",
    )(values, *before)


def rest_body(plus, minus, *refs):
    chips = (len(refs) - 7) // 1
    messages, keep, other, gathered = refs[:chips], refs[chips], refs[chips + 1], refs[chips + 2]
    scratch = refs[chips + 3 :]
    chip, core = place()
    for slot, message in enumerate(messages):
        base = 2 * jnp.bitwise_xor(chip, slot)
        gathered[base + core] = message[0]
        gathered[base + 1 - core] = message[1]
    convolve(lambda at: gathered[at], plus, minus, *scratch)
    acc_plus, acc_minus = scratch[2:]
    count, channels, span = gathered.shape
    half = count // 2
    gathered[:half] = (acc_plus[...] + acc_minus[...]).reshape(half, channels, span).astype(bf16)
    gathered[half:] = (acc_plus[...] - acc_minus[...]).reshape(half, channels, span).astype(bf16)
    for slot in range(chips):
        base = 2 * jnp.bitwise_xor(chip, slot)
        keep[slot] = gathered[base + core]
        other[slot] = gathered[base + 1 - core]


def convolve_rest(plus, minus, messages):
    chips = len(messages)
    _, channels, span = messages[0].shape
    result = shape_of((chips, channels, span))
    return pl.pallas_call(
        rest_body,
        out_shape=[result] * 2,
        in_specs=[VMEM] * (2 + chips),
        out_specs=[VMEM] * 2,
        scratch_shapes=[pltpu.VMEM((2 * chips, channels, span), bf16)]
        + scratch_for(2 * chips, channels, span),
        compiler_params=PARAMS,
        cost_estimate=cost(6e10, 1e8),
        name="conv_rest",
    )(plus, minus, *messages)


def join_body(keep, other, *messages):
    for slot, message in enumerate(messages):
        message[0] = keep[slot]
        message[1] = other[slot]


def join(keep, other):
    chips, channels, span = keep.shape
    return pl.pallas_call(
        join_body,
        out_shape=[shape_of((2, channels, span))] * chips,
        in_specs=[VMEM] * 2,
        out_specs=[VMEM] * chips,
        compiler_params=PARAMS,
        name="join",
    )(keep, other)


def mix_first_body(conv, gate, weight, out):
    devices, first, rows = conv.shape
    width = gate.shape[0]
    per = width // devices
    silu = gate[...].reshape(devices, per, rows)[:, :first]
    gated = (conv[...].astype(f32) * silu).astype(bf16).reshape(devices * first, rows)
    used = weight[...].reshape(devices, per, weight.shape[1])[:, :first]
    used = used.reshape(devices * first, weight.shape[1])
    out[...] = jnp.dot(gated.T, used, preferred_element_type=f32).astype(out.dtype)


def mix_first(conv, gate, weight, dtype):
    devices, first, rows = conv.shape
    return pl.pallas_call(
        mix_first_body,
        out_shape=shape_of((rows, weight.shape[1]), dtype),
        in_specs=[VMEM] * 3,
        out_specs=VMEM,
        compiler_params=PARAMS,
        cost_estimate=cost(2 * devices * first * rows * weight.shape[1], 8 * rows * weight.shape[1]),
        name="mix_first",
    )(conv, gate, weight)


def mix_rest_body(partial, gate, weight, *refs):
    messages, out, gathered = refs[:-2], refs[-2], refs[-1]
    devices, rest, rows = gathered.shape
    width = gate.shape[0]
    per = width // devices
    chip, core = place()
    for slot, message in enumerate(messages):
        base = 2 * jnp.bitwise_xor(chip, slot)
        gathered[base + core] = message[0]
        gathered[base + 1 - core] = message[1]
    silu = gate[...].reshape(devices, per, rows)[:, per - rest :]
    gated = (gathered[...].astype(f32) * silu).astype(bf16).reshape(devices * rest, rows)
    used = weight[...].reshape(devices, per, weight.shape[1])[:, per - rest :]
    used = used.reshape(devices * rest, weight.shape[1])
    total = partial[...] + jnp.dot(gated.T, used, preferred_element_type=f32)
    out[...] = total.astype(bf16)


def mix_rest(partial, gate, weight, messages):
    _, rest, rows = messages[0].shape
    devices = 2 * len(messages)
    return pl.pallas_call(
        mix_rest_body,
        out_shape=shape_of(partial.shape),
        in_specs=[VMEM] * (3 + len(messages)),
        out_specs=VMEM,
        scratch_shapes=[pltpu.VMEM((devices, rest, rows), bf16)],
        compiler_params=PARAMS,
        cost_estimate=cost(2 * devices * rest * rows * weight.shape[1], 8 * rows * weight.shape[1]),
        name="mix_rest",
    )(partial, gate, weight, *messages)


def to_core(block, devices):
    return lax.ppermute(block, "seq", [(i, i ^ 1) for i in range(devices)])


def to_chips(messages, devices):
    got = [messages[0]]
    for slot in range(1, len(messages)):
        got.append(lax.ppermute(messages[slot], "seq", [(i, i ^ (2 * slot)) for i in range(devices)]))
    return got


def body(tokens, value_weight, gate_weight, out_weight, kernel_weight, kernel_bias):
    rows, width = tokens.shape
    devices = lax.axis_size("seq")
    per = width // devices
    splits = per % (2 * TILE) == 0 and devices & (devices - 1) == 0
    first = per // 2 if splits else per
    blocks, *pair = project(tokens, value_weight, kernel_weight, kernel_bias, devices, first)
    columns = lax.all_to_all(blocks, "seq", split_axis=0, concat_axis=0, tiled=True)
    if splits:
        pair = [pair[0], to_core(pair[1], devices)]
    gate, *messages = gate_columns(tokens, gate_weight, pair)
    if splits:
        messages = to_chips(messages, devices)
    before = [] if splits else [gate]
    convolved, plus, minus = convolve_first(columns, first, rows, before)
    returned = lax.all_to_all(convolved, "seq", split_axis=0, concat_axis=0, tiled=True)
    if not splits:
        return mix_first(returned, gate, out_weight, bf16)
    keep, other = convolve_rest(plus, minus, messages)
    messages = to_chips(join(keep, to_core(other, devices)), devices)
    partial = mix_first(returned, gate, out_weight, f32)
    return mix_rest(partial, gate, out_weight, messages)


def solution(mesh):
    placed = (P(("grp", "seq"), None), P(), P(), P(), P(), P())
    return jax.shard_map(
        body, mesh=mesh, in_specs=placed, out_specs=P(("grp", "seq"), None), check_vma=False
    )
```

```python
import functools

import jax
import jax.numpy as jnp
from jax import lax
from jax.experimental import pallas as pl
from jax.experimental.pallas import tpu as pltpu
from jax.sharding import PartitionSpec as P

f32 = jnp.float32
bf16 = jnp.bfloat16
LANES = 128
TILE = 16
VMEM = pl.BlockSpec(memory_space=pltpu.VMEM)
HBM = pl.BlockSpec(memory_space=pltpu.HBM)
PARAMS = pltpu.CompilerParams(vmem_limit_bytes=48 * 2**20)
SMALL = pltpu.CompilerParams(vmem_limit_bytes=24 * 2**20)
LARGE = pltpu.CompilerParams(vmem_limit_bytes=62 * 2**20)


def cost(flops, nbytes):
    return pl.CostEstimate(flops=int(flops), bytes_accessed=int(nbytes), transcendentals=0)


def whole_block(shape):
    return pl.BlockSpec(shape, lambda i: (0,) * len(shape))


def shape_of(shape, dtype=bf16):
    return jax.ShapeDtypeStruct(shape, dtype)


def place():
    me = lax.axis_index("seq")
    return me // 2, lax.rem(me, 2)


def project_body(sizes, tokens, weight, lag_weight, lag_bias, *refs):
    devices, per, first, heads, pieces = sizes
    out, messages = refs[0], refs[1:-8]
    tokens_here, weight_here, out_here, rest_here, token_done, weight_done, out_done, rest_done = refs[-8:]
    rows, width = tokens.shape
    tiles = rows // LANES
    step = width // pieces
    count = step // per
    reading, writing = [], []
    for at in range(pieces):
        cut = (slice(None), slice(step * at, step * at + step))
        reading.append(pltpu.make_async_copy(weight.at[cut], weight_here.at[cut], weight_done.at[at]))
        cut = slice(count * at, count * at + count)
        writing.append(pltpu.make_async_copy(out_here.at[cut], out.at[cut], out_done.at[at]))
    token_copy = pltpu.make_async_copy(tokens, tokens_here, token_done.at[0])
    token_copy.start()
    reading[0].start()
    square = (heads, heads)
    on_line = lax.broadcasted_iota(jnp.int32, square, 0) == lax.broadcasted_iota(jnp.int32, square, 1)
    bias = jnp.sum(jnp.where(on_line, jnp.broadcast_to(lag_bias[...], square), 0.0), axis=1, keepdims=True)
    lag_columns = lag_weight[...].T
    token_copy.wait()
    for copy in reading[1:]:
        copy.start()
    logits = jnp.dot(tokens_here[...], lag_columns, preferred_element_type=f32).T + bias
    lag_rows = jnp.tanh(logits) * (rows * devices) ** (-0.5)
    chip, _ = place()
    for at in range(pieces):
        reading[at].wait()
        part = jnp.dot(
            tokens_here[...], weight_here[:, step * at : step * at + step], preferred_element_type=f32
        )
        part = part.astype(bf16).T
        for group in range(count):
            device = at * count + group
            block = part[per * group : per * group + first]
            for tile in range(tiles):
                out_here[device, first * tile : first * tile + first] = block[
                    :, LANES * tile : LANES * tile + LANES
                ]
            head = device * heads // devices
            row = lag_rows[head : head + 1]
            lines = [row[:, LANES * tile : LANES * tile + LANES] for tile in range(tiles)]
            lines.append(jnp.zeros((out.shape[1] - first * tiles - tiles, LANES), f32))
            out_here[device, first * tiles :] = jnp.concatenate(lines, axis=0).astype(bf16)
        writing[at].start()
        if first < per:
            for group in range(count):
                device = at * count + group
                slot = jnp.bitwise_xor(chip, device // 2)
                rest_here[slot, device % 2] = part[per * group + first : per * group + per]
    for slot, message in enumerate(messages):
        writing.append(pltpu.make_async_copy(rest_here.at[slot], message, rest_done.at[slot]))
        writing[-1].start()
    for copy in writing:
        copy.wait()


def project(tokens, weight, lag_weight, lag_bias, devices, first):
    rows, width = tokens.shape
    heads = lag_weight.shape[1]
    per = width // devices
    pieces = max(1, min(2, devices // 2))
    tall = first * (rows // LANES) + TILE
    outs = [shape_of((devices, tall, LANES))]
    if first < per:
        outs += [shape_of((2, per - first, rows))] * (devices // 2)
    return pl.pallas_call(
        functools.partial(project_body, (devices, per, first, heads, pieces)),
        out_shape=outs,
        in_specs=[HBM, HBM, VMEM, VMEM],
        out_specs=[HBM] * len(outs),
        scratch_shapes=[
            pltpu.VMEM((rows, width), bf16),
            pltpu.VMEM((width, width), bf16),
            pltpu.VMEM((devices, tall, LANES), bf16),
            pltpu.VMEM((devices // 2, 2, max(per - first, TILE), rows), bf16),
            pltpu.SemaphoreType.DMA((1,)),
            pltpu.SemaphoreType.DMA((pieces,)),
            pltpu.SemaphoreType.DMA((pieces,)),
            pltpu.SemaphoreType.DMA((devices // 2,)),
        ],
        compiler_params=LARGE,
        cost_estimate=cost(2 * rows * width * width, 4 * rows * width + 2 * width * width),
        name="project",
    )(tokens, weight, lag_weight.T, lag_bias.reshape(1, heads))


def fill_strips(row, plus, minus):
    length = row.shape[1]
    half = length // 2
    lead = plus.shape[1] - half
    low, high = row[:, :half] * 0.5, row[:, half:] * 0.5
    for ref, line, sign in ((plus, low + high, 1.0), (minus, low - high, -1.0)):
        for piece in range(LANES // TILE):
            turned = pltpu.roll(
                jnp.broadcast_to(line, (TILE, half)), TILE * piece, 1, stride=1, stride_axis=0
            )
            here = slice(TILE * piece, TILE * piece + TILE)
            edge = turned[:, :LANES]
            if sign < 0:
                down = lax.broadcasted_iota(jnp.int32, (TILE, LANES), 0) + TILE * piece
                across = lax.broadcasted_iota(jnp.int32, (TILE, LANES), 1)
                edge = jnp.where(across < down, -edge, edge)
            ref[here, :lead] = (turned[:, half - lead :] * sign).astype(bf16)
            ref[here, lead : lead + LANES] = edge.astype(bf16)
            ref[here, lead + LANES :] = turned[:, LANES:].astype(bf16)


def convolve(block_of, plus, minus, twice_plus, twice_minus, acc_plus, acc_minus):
    count, channels, span = twice_plus.shape
    half = count // 2
    lead = plus.shape[1] - half * span
    for at in range(half):
        low, high = block_of(at).astype(f32), block_of(at + half).astype(f32)
        total, gap = (low + high).astype(bf16), (low - high).astype(bf16)
        twice_plus[at] = total
        twice_plus[at + half] = total
        twice_minus[at] = -gap
        twice_minus[at + half] = gap
    group = min(half, 4)
    for acc, twice, strip in ((acc_plus, twice_plus, plus), (acc_minus, twice_minus, minus)):
        for start in range(0, half, group):
            left, right = [], []
            for lag in range(start, start + group):
                left.append(twice[half - lag : 2 * half - lag].reshape(half * channels, span))
                for part in range(span // LANES):
                    begin = span * lag + lead - LANES * part
                    right.append(strip[:, begin : begin + span])
            piece = jnp.dot(
                jnp.concatenate(left, axis=1), jnp.concatenate(right, axis=0), preferred_element_type=f32
            )
            acc[...] = piece if start == 0 else acc[...] + piece


def first_body(channels, values, *refs):
    out, lag_row, plus, minus, *scratch = refs
    count, tall, _ = values.shape
    span = out.shape[2]
    tiles = span // LANES
    pieces = []
    for at in range(count):
        rows = values[at, channels * tiles :].astype(f32)
        pieces += [rows[tile : tile + 1] for tile in range(tiles)]
    lag_row[...] = jnp.concatenate(pieces, axis=1)
    fill_strips(lag_row[...], plus, minus)

    def block_of(at):
        return jnp.concatenate(
            [values[at, channels * tile : channels * tile + channels] for tile in range(tiles)], axis=1
        )

    convolve(block_of, plus, minus, *scratch)
    acc_plus, acc_minus = scratch[2:]
    half = count // 2
    out[:half] = (acc_plus[...] + acc_minus[...]).reshape(half, channels, span).astype(bf16)
    out[half:] = (acc_plus[...] - acc_minus[...]).reshape(half, channels, span).astype(bf16)


def scratch_for(count, channels, span):
    return [pltpu.VMEM((LANES, count // 2 * span + span - LANES), bf16)] * 2 + [
        pltpu.VMEM((count, channels, span), bf16)
    ] * 2 + [
        pltpu.VMEM((count // 2 * channels, span), f32)
    ] * 2


def convolve_first(values, channels, span):
    count = values.shape[0]
    return pl.pallas_call(
        functools.partial(first_body, channels),
        out_shape=[shape_of((count, channels, span)), shape_of((1, count * span), f32)],
        in_specs=[VMEM],
        out_specs=[VMEM] * 2,
        scratch_shapes=scratch_for(count, channels, span),
        compiler_params=SMALL,
        cost_estimate=cost(1e6, 1e5),
        name="conv_first",
    )(values)


def pack_body(chips, *refs):
    messages, out, done = refs[:chips], refs[-2], refs[-1]
    core = 1 - place()[1]
    copies = [
        pltpu.make_async_copy(messages[slot].at[core], out.at[slot], done.at[slot]) for slot in range(chips)
    ]
    for copy in copies:
        copy.start()
    for copy in copies:
        copy.wait()


def pack(messages, after):
    chips = len(messages)
    return pl.pallas_call(
        functools.partial(pack_body, chips),
        out_shape=shape_of((chips,) + messages[0].shape[1:]),
        in_specs=[HBM] * (chips + 1),
        out_specs=VMEM,
        scratch_shapes=[pltpu.SemaphoreType.DMA((chips,))],
        compiler_params=SMALL,
        cost_estimate=cost(6e10, 1e8),
        name="pack",
    )(*messages, after)


def rest_body(lag_row, crossed, *refs):
    chips = len(refs) - 10
    messages, keep, other = refs[:chips], refs[chips], refs[chips + 1]
    gathered, done, *scratch = refs[chips + 2 :]
    plus, minus = scratch[:2]
    chip, core = place()
    copies = []
    for slot, message in enumerate(messages):
        base = 2 * jnp.bitwise_xor(chip, slot)
        copies.append(pltpu.make_async_copy(message.at[core], gathered.at[base + core], done.at[slot]))
        copies[-1].start()
    fill_strips(lag_row[...], plus, minus)
    for slot in range(chips):
        gathered[2 * jnp.bitwise_xor(chip, slot) + 1 - core] = crossed[slot]
    for copy in copies:
        copy.wait()
    convolve(lambda at: gathered[at], *scratch)
    acc_plus, acc_minus = scratch[4:]
    count, channels, span = gathered.shape
    half = count // 2
    gathered[:half] = (acc_plus[...] + acc_minus[...]).reshape(half, channels, span).astype(bf16)
    gathered[half:] = (acc_plus[...] - acc_minus[...]).reshape(half, channels, span).astype(bf16)
    for slot in range(chips):
        base = 2 * jnp.bitwise_xor(chip, slot)
        keep[slot] = gathered[base + core]
        other[slot] = gathered[base + 1 - core]


def convolve_rest(lag_row, crossed, messages):
    chips = len(messages)
    _, channels, span = messages[0].shape
    result = shape_of((chips, channels, span))
    return pl.pallas_call(
        rest_body,
        out_shape=[result] * 2,
        in_specs=[VMEM] * 2 + [HBM] * chips,
        out_specs=[VMEM] * 2,
        scratch_shapes=[pltpu.VMEM((2 * chips, channels, span), bf16), pltpu.SemaphoreType.DMA((chips,))]
        + scratch_for(2 * chips, channels, span),
        compiler_params=SMALL,
        cost_estimate=cost(1e6, 1e5),
        name="conv_rest",
    )(lag_row, crossed, *messages)


def join_body(keep, other, *messages):
    for slot, message in enumerate(messages):
        message[0] = keep[slot]
        message[1] = other[slot]


def join(keep, other):
    chips, channels, span = keep.shape
    return pl.pallas_call(
        join_body,
        out_shape=[shape_of((2, channels, span))] * chips,
        in_specs=[VMEM] * 2,
        out_specs=[VMEM] * chips,
        compiler_params=SMALL,
        name="join",
    )(keep, other)


def mix_first_body(tokens, gate_weight, conv, weight, out, *late):
    devices, first, rows = conv.shape
    width, columns = weight.shape
    per = width // devices
    gate = jnp.dot(tokens[...], gate_weight[...], preferred_element_type=f32)
    silu = (gate / (1.0 + jnp.exp(-gate))).T.reshape(devices, per, rows)
    used = weight[...].reshape(devices, per, columns)
    gated = (conv[...].astype(f32) * silu[:, :first]).astype(bf16).reshape(devices * first, rows)
    mixed = jnp.dot(
        gated.T, used[:, :first].reshape(devices * first, columns), preferred_element_type=f32
    )
    out[...] = mixed.astype(out.dtype)
    if late:
        late[0][...] = silu[:, first:]
        late[1][...] = used[:, first:]


def mix_first(tokens, gate_weight, conv, weight):
    devices, first, rows = conv.shape
    width, columns = weight.shape
    rest = width // devices - first
    outs = [shape_of((rows, columns), f32 if rest else bf16)]
    if rest:
        outs += [shape_of((devices, rest, rows), f32), shape_of((devices, rest, columns))]
    return pl.pallas_call(
        mix_first_body,
        out_shape=outs,
        in_specs=[VMEM] * 4,
        out_specs=[VMEM] * len(outs),
        compiler_params=SMALL,
        cost_estimate=cost(4 * width * rows * columns, 8 * rows * columns),
        name="mix_first",
    )(tokens, gate_weight, conv, weight)


def mix_rest_body(partial, silu, weight, *refs):
    messages, out, gathered = refs[:-2], refs[-2], refs[-1]
    devices, rest, rows = gathered.shape
    chip, core = place()
    for slot, message in enumerate(messages):
        base = 2 * jnp.bitwise_xor(chip, slot)
        gathered[base + core] = message[0]
        gathered[base + 1 - core] = message[1]
    gated = (gathered[...].astype(f32) * silu[...]).astype(bf16).reshape(devices * rest, rows)
    used = weight[...].reshape(devices * rest, weight.shape[2])
    total = partial[...] + jnp.dot(gated.T, used, preferred_element_type=f32)
    out[...] = total.astype(bf16)


def mix_rest(partial, silu, weight, messages):
    devices, rest, rows = silu.shape
    return pl.pallas_call(
        mix_rest_body,
        out_shape=shape_of(partial.shape),
        in_specs=[VMEM] * (3 + len(messages)),
        out_specs=VMEM,
        scratch_shapes=[pltpu.VMEM((devices, rest, rows), bf16)],
        compiler_params=SMALL,
        cost_estimate=cost(2 * devices * rest * rows * weight.shape[2], 8 * rows * weight.shape[2]),
        name="mix_rest",
    )(partial, silu, weight, *messages)


def to_core(block, devices):
    return lax.ppermute(block, "seq", [(i, i ^ 1) for i in range(devices)])


def to_chips(messages, devices):
    got = [messages[0]]
    for slot in range(1, len(messages)):
        got.append(lax.ppermute(messages[slot], "seq", [(i, i ^ (2 * slot)) for i in range(devices)]))
    return got


def body(tokens, value_weight, gate_weight, out_weight, kernel_weight, kernel_bias):
    rows, width = tokens.shape
    devices = lax.axis_size("seq")
    per = width // devices
    splits = per % (2 * TILE) == 0 and devices & (devices - 1) == 0
    first = per // 2 if splits else per
    blocks, *rest = project(tokens, value_weight, kernel_weight, kernel_bias, devices, first)
    columns = lax.all_to_all(blocks, "seq", split_axis=0, concat_axis=0, tiled=True)
    if splits:
        messages = to_chips(rest, devices)
    convolved, lag_row = convolve_first(columns, first, rows)
    returned = lax.all_to_all(convolved, "seq", split_axis=0, concat_axis=0, tiled=True)
    if not splits:
        return mix_first(tokens, gate_weight, returned, out_weight)[0]
    crossed = to_core(pack(messages, lag_row), devices)
    keep, other = convolve_rest(lag_row, crossed, messages)
    messages = to_chips(join(keep, to_core(other, devices)), devices)
    return mix_rest(*mix_first(tokens, gate_weight, returned, out_weight), messages)


def solution(mesh):
    placed = (P(("grp", "seq"), None), P(), P(), P(), P(), P())
    return jax.shard_map(
        body, mesh=mesh, in_specs=placed, out_specs=P(("grp", "seq"), None), check_vma=False
    )
```

```python
import functools

import jax
import jax.numpy as jnp
from jax import lax
from jax.experimental import pallas as pl
from jax.experimental.pallas import tpu as pltpu
from jax.sharding import PartitionSpec as P

f32 = jnp.float32
bf16 = jnp.bfloat16
LANES = 128
TILE = 16
VMEM = pl.BlockSpec(memory_space=pltpu.VMEM)
HBM = pl.BlockSpec(memory_space=pltpu.HBM)
PARAMS = pltpu.CompilerParams(vmem_limit_bytes=48 * 2**20)
SMALL = pltpu.CompilerParams(vmem_limit_bytes=24 * 2**20)
LARGE = pltpu.CompilerParams(vmem_limit_bytes=62 * 2**20)


def cost(flops, nbytes):
    return pl.CostEstimate(flops=int(flops), bytes_accessed=int(nbytes), transcendentals=0)


def whole_block(shape):
    return pl.BlockSpec(shape, lambda i: (0,) * len(shape))


def shape_of(shape, dtype=bf16):
    return jax.ShapeDtypeStruct(shape, dtype)


def place():
    me = lax.axis_index("seq")
    return me // 2, lax.rem(me, 2)


def load(tokens, weight, cuts, tokens_here, weight_here, done):
    copies = [pltpu.make_async_copy(tokens, tokens_here, done.at[0])]
    at = 0
    for number, (start, size) in enumerate(cuts):
        copies.append(
            pltpu.make_async_copy(
                weight.at[:, start : start + size], weight_here.at[:, at : at + size], done.at[number + 1]
            )
        )
        at += size
    return copies


def load_scratch(rows, width, cuts):
    return [
        pltpu.VMEM((rows, width), bf16),
        pltpu.VMEM((width, sum(size for _, size in cuts)), bf16),
        pltpu.SemaphoreType.DMA((len(cuts) + 1,)),
    ]


def first_project_body(devices, channels, cuts, heads_of, tokens, weight, lag_weight, lag_bias, out, *refs):
    tokens_here, weight_here, done, out_here, out_done = refs
    rows = tokens.shape[0]
    heads = lag_weight.shape[0]
    tiles = rows // LANES
    copies = load(tokens, weight, cuts, tokens_here, weight_here, done)
    for copy in copies:
        copy.start()
    square = (heads, heads)
    on_line = lax.broadcasted_iota(jnp.int32, square, 0) == lax.broadcasted_iota(jnp.int32, square, 1)
    bias = jnp.sum(jnp.where(on_line, jnp.broadcast_to(lag_bias[...], square), 0.0), axis=1, keepdims=True)
    lag_columns = lag_weight[...].T
    copies[0].wait()
    logits = jnp.dot(tokens_here[...], lag_columns, preferred_element_type=f32).T + bias
    lag_rows = jnp.tanh(logits) * (rows * devices) ** (-0.5)
    for copy in copies[1:]:
        copy.wait()
    part = jnp.dot(tokens_here[...], weight_here[...], preferred_element_type=f32).astype(bf16).T
    writing = []
    half = devices // 2
    for device in range(devices):
        block = part[channels * device : channels * device + channels]
        for tile in range(tiles):
            out_here[device, channels * tile : channels * tile + channels] = block[
                :, LANES * tile : LANES * tile + LANES
            ]
        lines = []
        for head in heads_of[device]:
            row = lag_rows[head : head + 1]
            lines += [row[:, LANES * tile : LANES * tile + LANES] for tile in range(tiles)]
        left = out.shape[1] - channels * tiles - len(lines)
        if left:
            lines.append(jnp.zeros((left, LANES), f32))
        out_here[device, channels * tiles :] = jnp.concatenate(lines, axis=0).astype(bf16)
        if device % half == half - 1:
            cut = slice(device + 1 - half, device + 1)
            writing.append(pltpu.make_async_copy(out_here.at[cut], out.at[cut], out_done.at[device // half]))
            writing[-1].start()
    for copy in writing:
        copy.wait()


def first_project(tokens, weight, lag_weight, lag_bias, devices, channels, cuts, heads_of):
    rows, width = tokens.shape
    heads = lag_weight.shape[1]
    out = (devices, channels * (rows // LANES) + 8, LANES)
    return pl.pallas_call(
        functools.partial(first_project_body, devices, channels, cuts, heads_of),
        out_shape=shape_of(out),
        in_specs=[HBM, HBM, VMEM, VMEM],
        out_specs=HBM,
        scratch_shapes=load_scratch(rows, width, cuts)
        + [pltpu.VMEM(out, bf16), pltpu.SemaphoreType.DMA((2,))],
        compiler_params=LARGE,
        cost_estimate=cost(2 * rows * width * width, 4 * rows * width + 2 * width * width),
        name="project_first",
    )(tokens, weight, lag_weight.T, lag_bias.reshape(1, heads))


def rest_project_body(channels, cuts, tokens, weight, keep, other, *refs):
    tokens_here, weight_here, done = refs
    copies = load(tokens, weight, cuts, tokens_here, weight_here, done)
    for copy in copies:
        copy.start()
    for copy in copies:
        copy.wait()
    part = jnp.dot(tokens_here[...], weight_here[...], preferred_element_type=f32).astype(bf16).T
    chip, core = place()
    for there in range(keep.shape[0]):
        low = part[2 * channels * there : 2 * channels * there + channels]
        high = part[2 * channels * there + channels : 2 * channels * there + 2 * channels]
        slot = jnp.bitwise_xor(chip, there)
        keep[slot] = jnp.where(core == 0, low, high)
        other[slot] = jnp.where(core == 0, high, low)


def rest_project(tokens, weight, chips, channels, cuts):
    rows, width = tokens.shape
    half = (chips, channels, rows)
    return pl.pallas_call(
        functools.partial(rest_project_body, channels, cuts),
        out_shape=[shape_of(half)] * 2,
        in_specs=[HBM, HBM],
        out_specs=[VMEM] * 2,
        scratch_shapes=load_scratch(rows, width, cuts),
        compiler_params=SMALL,
        cost_estimate=cost(rows * width * width, 4 * rows * width),
        name="project_rest",
    )(tokens, weight)


def meet_body(keep, other, *messages):
    _, core = place()
    for slot, message in enumerate(messages):
        message[core] = keep[slot]
        message[1 - core] = other[slot]


def meet(keep, other):
    chips, channels, rows = keep.shape
    return pl.pallas_call(
        meet_body,
        out_shape=[shape_of((2, channels, rows))] * chips,
        in_specs=[VMEM] * 2,
        out_specs=[VMEM] * chips,
        compiler_params=SMALL,
        name="meet",
    )(keep, other)


def fill_strips(row, plus, minus):
    length = row.shape[1]
    half = length // 2
    lead = plus.shape[1] - half
    low, high = row[:, :half] * 0.5, row[:, half:] * 0.5
    for ref, line, sign in ((plus, low + high, 1.0), (minus, low - high, -1.0)):
        for piece in range(LANES // TILE):
            turned = pltpu.roll(
                jnp.broadcast_to(line, (TILE, half)), TILE * piece, 1, stride=1, stride_axis=0
            )
            here = slice(TILE * piece, TILE * piece + TILE)
            edge = turned[:, :LANES]
            if sign < 0:
                down = lax.broadcasted_iota(jnp.int32, (TILE, LANES), 0) + TILE * piece
                across = lax.broadcasted_iota(jnp.int32, (TILE, LANES), 1)
                edge = jnp.where(across < down, -edge, edge)
            ref[here, :lead] = (turned[:, half - lead :] * sign).astype(bf16)
            ref[here, lead : lead + LANES] = edge.astype(bf16)
            ref[here, lead + LANES :] = turned[:, LANES:].astype(bf16)


def convolve(block_of, plus, minus, twice_plus, twice_minus, acc_plus, acc_minus):
    count, channels, span = twice_plus.shape
    half = count // 2
    lead = plus.shape[1] - half * span
    for at in range(half):
        low, high = block_of(at).astype(f32), block_of(at + half).astype(f32)
        total, gap = (low + high).astype(bf16), (low - high).astype(bf16)
        twice_plus[at] = total
        twice_plus[at + half] = total
        twice_minus[at] = -gap
        twice_minus[at + half] = gap
    group = min(half, 4)
    for acc, twice, strip in ((acc_plus, twice_plus, plus), (acc_minus, twice_minus, minus)):
        for start in range(0, half, group):
            left, right = [], []
            for lag in range(start, start + group):
                left.append(twice[half - lag : 2 * half - lag].reshape(half * channels, span))
                for part in range(span // LANES):
                    begin = span * lag + lead - LANES * part
                    right.append(strip[:, begin : begin + span])
            piece = jnp.dot(
                jnp.concatenate(left, axis=1), jnp.concatenate(right, axis=0), preferred_element_type=f32
            )
            acc[...] = piece if start == 0 else acc[...] + piece


def first_body(channels, values, *refs):
    out, lag_row, plus, minus, *scratch = refs
    count, tall, _ = values.shape
    span = out.shape[2]
    tiles = span // LANES
    own, later = [], []
    for at in range(count):
        rows = values[at, channels * tiles :].astype(f32)
        own += [rows[tile : tile + 1] for tile in range(tiles)]
        later += [rows[tiles + tile : tiles + tile + 1] for tile in range(tiles)]
    lag_row[...] = jnp.concatenate(later, axis=1)
    fill_strips(jnp.concatenate(own, axis=1), plus, minus)

    def block_of(at):
        return jnp.concatenate(
            [values[at, channels * tile : channels * tile + channels] for tile in range(tiles)], axis=1
        )

    convolve(block_of, plus, minus, *scratch)
    acc_plus, acc_minus = scratch[2:]
    half = count // 2
    out[:half] = (acc_plus[...] + acc_minus[...]).reshape(half, channels, span).astype(bf16)
    out[half:] = (acc_plus[...] - acc_minus[...]).reshape(half, channels, span).astype(bf16)


def scratch_for(count, channels, span):
    return [pltpu.VMEM((LANES, count // 2 * span + span - LANES), bf16)] * 2 + [
        pltpu.VMEM((count, channels, span), bf16)
    ] * 2 + [
        pltpu.VMEM((count // 2 * channels, span), f32)
    ] * 2


def convolve_first(values, channels, span):
    count = values.shape[0]
    return pl.pallas_call(
        functools.partial(first_body, channels),
        out_shape=[shape_of((count, channels, span)), shape_of((1, count * span), f32)],
        in_specs=[VMEM],
        out_specs=[VMEM] * 2,
        scratch_shapes=scratch_for(count, channels, span),
        compiler_params=SMALL,
        cost_estimate=cost(1e6, 1e5),
        name="conv_first",
    )(values)


def rest_body(lag_row, *refs):
    chips = len(refs) - 10
    messages, keep, other = refs[:chips], refs[chips], refs[chips + 1]
    gathered, done, *scratch = refs[chips + 2 :]
    plus, minus = scratch[:2]
    chip, core = place()
    copies = []
    for slot, message in enumerate(messages):
        base = 2 * jnp.bitwise_xor(chip, slot)
        copies.append(pltpu.make_async_copy(message, gathered.at[pl.ds(base, 2)], done.at[slot]))
        copies[-1].start()
    fill_strips(lag_row[...], plus, minus)
    for copy in copies:
        copy.wait()
    convolve(lambda at: gathered[at], *scratch)
    acc_plus, acc_minus = scratch[4:]
    count, channels, span = gathered.shape
    half = count // 2
    gathered[:half] = (acc_plus[...] + acc_minus[...]).reshape(half, channels, span).astype(bf16)
    gathered[half:] = (acc_plus[...] - acc_minus[...]).reshape(half, channels, span).astype(bf16)
    for slot in range(chips):
        base = 2 * jnp.bitwise_xor(chip, slot)
        keep[slot] = gathered[base + core]
        other[slot] = gathered[base + 1 - core]


def convolve_rest(lag_row, messages):
    chips = len(messages)
    _, channels, span = messages[0].shape
    result = shape_of((chips, channels, span))
    return pl.pallas_call(
        rest_body,
        out_shape=[result] * 2,
        in_specs=[VMEM] + [HBM] * chips,
        out_specs=[VMEM] * 2,
        scratch_shapes=[pltpu.VMEM((2 * chips, channels, span), bf16), pltpu.SemaphoreType.DMA((chips,))]
        + scratch_for(2 * chips, channels, span),
        compiler_params=SMALL,
        cost_estimate=cost(6e10, 1e8),
        name="conv_rest",
    )(lag_row, *messages)


def join_body(keep, other, *messages):
    for slot, message in enumerate(messages):
        message[0] = keep[slot]
        message[1] = other[slot]


def join(keep, other):
    chips, channels, span = keep.shape
    return pl.pallas_call(
        join_body,
        out_shape=[shape_of((2, channels, span))] * chips,
        in_specs=[VMEM] * 2,
        out_specs=[VMEM] * chips,
        compiler_params=SMALL,
        name="join",
    )(keep, other)


def mix_first_body(tokens, gate_weight, conv, weight, out, *late):
    devices, first, rows = conv.shape
    width, columns = weight.shape
    per = width // devices
    gate = jnp.dot(tokens[...], gate_weight[...], preferred_element_type=f32)
    silu = (gate / (1.0 + jnp.exp(-gate))).T
    used = weight[...]
    if late:
        silu = silu.reshape(devices // 4, 4 * per, rows)
        used = used.reshape(devices // 4, 4 * per, columns)
        late[0][...] = silu[:, 4 * first :].reshape(late[0].shape)
        late[1][...] = used[:, 4 * first :].reshape(late[1].shape)
        silu = silu[:, : 4 * first]
        used = used[:, : 4 * first].reshape(devices * first, columns)
    gated = (conv[...].astype(f32) * silu.reshape(devices, first, rows)).astype(bf16)
    mixed = jnp.dot(gated.reshape(devices * first, rows).T, used, preferred_element_type=f32)
    out[...] = mixed.astype(out.dtype)


def mix_first(tokens, gate_weight, conv, weight):
    devices, first, rows = conv.shape
    width, columns = weight.shape
    rest = width // devices - first
    outs = [shape_of((rows, columns), f32 if rest else bf16)]
    if rest:
        outs += [shape_of((devices, rest, rows), f32), shape_of((devices, rest, columns))]
    return pl.pallas_call(
        mix_first_body,
        out_shape=outs,
        in_specs=[VMEM] * 4,
        out_specs=[VMEM] * len(outs),
        compiler_params=SMALL,
        cost_estimate=cost(4 * width * rows * columns, 8 * rows * columns),
        name="mix_first",
    )(tokens, gate_weight, conv, weight)


def mix_rest_body(partial, silu, weight, *refs):
    messages, out, gathered = refs[:-2], refs[-2], refs[-1]
    devices, rest, rows = gathered.shape
    chip, core = place()
    for slot, message in enumerate(messages):
        base = 2 * jnp.bitwise_xor(chip, slot)
        gathered[base + core] = message[0]
        gathered[base + 1 - core] = message[1]
    gated = (gathered[...].astype(f32) * silu[...]).astype(bf16).reshape(devices * rest, rows)
    used = weight[...].reshape(devices * rest, weight.shape[2])
    total = partial[...] + jnp.dot(gated.T, used, preferred_element_type=f32)
    out[...] = total.astype(bf16)


def mix_rest(partial, silu, weight, messages):
    devices, rest, rows = silu.shape
    return pl.pallas_call(
        mix_rest_body,
        out_shape=shape_of(partial.shape),
        in_specs=[VMEM] * (3 + len(messages)),
        out_specs=VMEM,
        scratch_shapes=[pltpu.VMEM((devices, rest, rows), bf16)],
        compiler_params=SMALL,
        cost_estimate=cost(2 * devices * rest * rows * weight.shape[2], 8 * rows * weight.shape[2]),
        name="mix_rest",
    )(partial, silu, weight, *messages)


def to_core(block, devices):
    return lax.ppermute(block, "seq", [(i, i ^ 1) for i in range(devices)])


def to_chips(messages, devices):
    got = [messages[0]]
    for slot in range(1, len(messages)):
        got.append(lax.ppermute(messages[slot], "seq", [(i, i ^ (2 * slot)) for i in range(devices)]))
    return got


def body(tokens, value_weight, gate_weight, out_weight, kernel_weight, kernel_bias):
    rows, width = tokens.shape
    devices = lax.axis_size("seq")
    per = width // devices
    heads = kernel_weight.shape[1]
    splits = per % (2 * TILE) == 0 and devices & (devices - 1) == 0 and devices % 4 == 0
    splits = splits and heads == devices and 2 * per % LANES == 0
    if splits:
        first = per // 2
        span = 4 * per
        cuts = [(span * at, span // 2) for at in range(devices // 4)]
        later = [(start + size, size) for start, size in cuts]
        pairs = [(at // 4 * 4 + at % 4 // 2, at // 4 * 4 + 2 + at % 4 // 2) for at in range(devices)]
        blocks = first_project(
            tokens, value_weight, kernel_weight, kernel_bias, devices, first, cuts, pairs
        )
    else:
        first = per
        alone = [(at * heads // devices,) for at in range(devices)]
        blocks = first_project(
            tokens, value_weight, kernel_weight, kernel_bias, devices, first, [(0, width)], alone
        )
    columns = lax.all_to_all(blocks, "seq", split_axis=0, concat_axis=0, tiled=True)
    if splits:
        keep, other = rest_project(tokens, value_weight, devices // 2, per - first, later)
        messages = to_chips(meet(keep, to_core(other, devices)), devices)
    convolved, lag_row = convolve_first(columns, first, rows)
    returned = lax.all_to_all(convolved, "seq", split_axis=0, concat_axis=0, tiled=True)
    if not splits:
        return mix_first(tokens, gate_weight, returned, out_weight)[0]
    keep, other = convolve_rest(lag_row, messages)
    messages = to_chips(join(keep, to_core(other, devices)), devices)
    return mix_rest(*mix_first(tokens, gate_weight, returned, out_weight), messages)


def solution(mesh):
    placed = (P(("grp", "seq"), None), P(), P(), P(), P(), P())
    return jax.shard_map(
        body, mesh=mesh, in_specs=placed, out_specs=P(("grp", "seq"), None), check_vma=False
    )
```

```python
import functools

import jax
import jax.numpy as jnp
from jax import lax
from jax.experimental import pallas as pl
from jax.experimental.pallas import tpu as pltpu
from jax.sharding import PartitionSpec as P

f32 = jnp.float32
bf16 = jnp.bfloat16
LANES = 128
TILE = 16
VMEM = pl.BlockSpec(memory_space=pltpu.VMEM)
HBM = pl.BlockSpec(memory_space=pltpu.HBM)
PARAMS = pltpu.CompilerParams(vmem_limit_bytes=48 * 2**20)
SMALL = pltpu.CompilerParams(vmem_limit_bytes=24 * 2**20)
LARGE = pltpu.CompilerParams(vmem_limit_bytes=62 * 2**20)


def cost(flops, nbytes):
    return pl.CostEstimate(flops=int(flops), bytes_accessed=int(nbytes), transcendentals=0)


def whole_block(shape):
    return pl.BlockSpec(shape, lambda i: (0,) * len(shape))


def shape_of(shape, dtype=bf16):
    return jax.ShapeDtypeStruct(shape, dtype)


def place():
    me = lax.axis_index("seq")
    return me // 2, lax.rem(me, 2)


def load(tokens, weight, cuts, tokens_here, weight_here, done):
    copies = [pltpu.make_async_copy(tokens, tokens_here, done.at[0])]
    at = 0
    for number, (start, size) in enumerate(cuts):
        copies.append(
            pltpu.make_async_copy(
                weight.at[:, start : start + size], weight_here.at[:, at : at + size], done.at[number + 1]
            )
        )
        at += size
    return copies


def load_scratch(rows, width, cuts):
    return [
        pltpu.VMEM((rows, width), bf16),
        pltpu.VMEM((width, sum(size for _, size in cuts)), bf16),
        pltpu.SemaphoreType.DMA((len(cuts) + 1,)),
    ]


def first_project_body(devices, channels, cuts, heads_of, tokens, weight, lag_weight, lag_bias, out, *refs):
    tokens_here, weight_here, done, out_here, out_done = refs
    rows = tokens.shape[0]
    heads = lag_weight.shape[0]
    tiles = rows // LANES
    copies = load(tokens, weight, cuts, tokens_here, weight_here, done)
    for copy in copies:
        copy.start()
    square = (heads, heads)
    on_line = lax.broadcasted_iota(jnp.int32, square, 0) == lax.broadcasted_iota(jnp.int32, square, 1)
    bias = jnp.sum(jnp.where(on_line, jnp.broadcast_to(lag_bias[...], square), 0.0), axis=1, keepdims=True)
    lag_columns = lag_weight[...].T
    copies[0].wait()
    logits = jnp.dot(tokens_here[...], lag_columns, preferred_element_type=f32).T + bias
    lag_rows = jnp.tanh(logits) * (rows * devices) ** (-0.5)
    for copy in copies[1:]:
        copy.wait()
    part = jnp.dot(tokens_here[...], weight_here[...], preferred_element_type=f32).astype(bf16).T
    writing = []
    half = devices // 2
    for device in range(devices):
        block = part[channels * device : channels * device + channels]
        for tile in range(tiles):
            out_here[device, channels * tile : channels * tile + channels] = block[
                :, LANES * tile : LANES * tile + LANES
            ]
        lines = []
        for head in heads_of[device]:
            row = lag_rows[head : head + 1]
            lines += [row[:, LANES * tile : LANES * tile + LANES] for tile in range(tiles)]
        left = out.shape[1] - channels * tiles - len(lines)
        if left:
            lines.append(jnp.zeros((left, LANES), f32))
        out_here[device, channels * tiles :] = jnp.concatenate(lines, axis=0).astype(bf16)
        if device % half == half - 1:
            cut = slice(device + 1 - half, device + 1)
            writing.append(pltpu.make_async_copy(out_here.at[cut], out.at[cut], out_done.at[device // half]))
            writing[-1].start()
    for copy in writing:
        copy.wait()


def first_project(tokens, weight, lag_weight, lag_bias, devices, channels, cuts, heads_of):
    rows, width = tokens.shape
    heads = lag_weight.shape[1]
    out = (devices, channels * (rows // LANES) + 8, LANES)
    return pl.pallas_call(
        functools.partial(first_project_body, devices, channels, cuts, heads_of),
        out_shape=shape_of(out),
        in_specs=[HBM, HBM, VMEM, VMEM],
        out_specs=HBM,
        scratch_shapes=load_scratch(rows, width, cuts)
        + [pltpu.VMEM(out, bf16), pltpu.SemaphoreType.DMA((2,))],
        compiler_params=LARGE,
        cost_estimate=cost(2 * rows * width * width, 4 * rows * width + 2 * width * width),
        name="project_first",
    )(tokens, weight, lag_weight.T, lag_bias.reshape(1, heads))


def rest_project_body(channels, cuts, tokens, weight, keep, other, *refs):
    tokens_here, weight_here, done = refs
    copies = load(tokens, weight, cuts, tokens_here, weight_here, done)
    for copy in copies:
        copy.start()
    for copy in copies:
        copy.wait()
    part = jnp.dot(tokens_here[...], weight_here[...], preferred_element_type=f32).astype(bf16).T
    chip, core = place()
    for there in range(keep.shape[0]):
        low = part[2 * channels * there : 2 * channels * there + channels]
        high = part[2 * channels * there + channels : 2 * channels * there + 2 * channels]
        slot = jnp.bitwise_xor(chip, there)
        keep[slot] = jnp.where(core == 0, low, high)
        other[slot] = jnp.where(core == 0, high, low)


def rest_project(tokens, weight, chips, channels, cuts):
    rows, width = tokens.shape
    half = (chips, channels, rows)
    return pl.pallas_call(
        functools.partial(rest_project_body, channels, cuts),
        out_shape=[shape_of(half)] * 2,
        in_specs=[HBM, HBM],
        out_specs=[VMEM] * 2,
        scratch_shapes=load_scratch(rows, width, cuts),
        compiler_params=SMALL,
        cost_estimate=cost(rows * width * width, 4 * rows * width),
        name="project_rest",
    )(tokens, weight)


def meet_body(keep, other, *messages):
    _, core = place()
    for slot, message in enumerate(messages):
        message[core] = keep[slot]
        message[1 - core] = other[slot]


def meet(keep, other):
    chips, channels, rows = keep.shape
    return pl.pallas_call(
        meet_body,
        out_shape=[shape_of((2, channels, rows))] * chips,
        in_specs=[VMEM] * 2,
        out_specs=[VMEM] * chips,
        compiler_params=SMALL,
        name="meet",
    )(keep, other)


def fill_strips(row, plus, minus):
    length = row.shape[1]
    half = length // 2
    lead = plus.shape[1] - half
    low, high = row[:, :half] * 0.5, row[:, half:] * 0.5
    for ref, line, sign in ((plus, low + high, 1.0), (minus, low - high, -1.0)):
        for piece in range(LANES // TILE):
            turned = pltpu.roll(
                jnp.broadcast_to(line, (TILE, half)), TILE * piece, 1, stride=1, stride_axis=0
            )
            here = slice(TILE * piece, TILE * piece + TILE)
            edge = turned[:, :LANES]
            if sign < 0:
                down = lax.broadcasted_iota(jnp.int32, (TILE, LANES), 0) + TILE * piece
                across = lax.broadcasted_iota(jnp.int32, (TILE, LANES), 1)
                edge = jnp.where(across < down, -edge, edge)
            ref[here, :lead] = (turned[:, half - lead :] * sign).astype(bf16)
            ref[here, lead : lead + LANES] = edge.astype(bf16)
            ref[here, lead + LANES :] = turned[:, LANES:].astype(bf16)


def convolve(block_of, plus, minus, twice_plus, twice_minus, acc_plus, acc_minus):
    count, channels, span = twice_plus.shape
    half = count // 2
    lead = plus.shape[1] - half * span
    for at in range(half):
        low, high = block_of(at).astype(f32), block_of(at + half).astype(f32)
        total, gap = (low + high).astype(bf16), (low - high).astype(bf16)
        twice_plus[at] = total
        twice_plus[at + half] = total
        twice_minus[at] = -gap
        twice_minus[at + half] = gap
    group = min(half, 4)
    for acc, twice, strip in ((acc_plus, twice_plus, plus), (acc_minus, twice_minus, minus)):
        for start in range(0, half, group):
            left, right = [], []
            for lag in range(start, start + group):
                left.append(twice[half - lag : 2 * half - lag].reshape(half * channels, span))
                for part in range(span // LANES):
                    begin = span * lag + lead - LANES * part
                    right.append(strip[:, begin : begin + span])
            piece = jnp.dot(
                jnp.concatenate(left, axis=1), jnp.concatenate(right, axis=0), preferred_element_type=f32
            )
            acc[...] = piece if start == 0 else acc[...] + piece


def first_body(channels, values, *refs):
    out, lag_row, plus, minus, *scratch = refs
    count, tall, _ = values.shape
    span = out.shape[2]
    tiles = span // LANES
    own, later = [], []
    for at in range(count):
        rows = values[at, channels * tiles :].astype(f32)
        own += [rows[tile : tile + 1] for tile in range(tiles)]
        later += [rows[tiles + tile : tiles + tile + 1] for tile in range(tiles)]
    lag_row[...] = jnp.concatenate(later, axis=1)
    fill_strips(jnp.concatenate(own, axis=1), plus, minus)

    def block_of(at):
        return jnp.concatenate(
            [values[at, channels * tile : channels * tile + channels] for tile in range(tiles)], axis=1
        )

    convolve(block_of, plus, minus, *scratch)
    acc_plus, acc_minus = scratch[2:]
    half = count // 2
    out[:half] = (acc_plus[...] + acc_minus[...]).reshape(half, channels, span).astype(bf16)
    out[half:] = (acc_plus[...] - acc_minus[...]).reshape(half, channels, span).astype(bf16)


def scratch_for(count, channels, span):
    return [pltpu.VMEM((LANES, count // 2 * span + span - LANES), bf16)] * 2 + [
        pltpu.VMEM((count, channels, span), bf16)
    ] * 2 + [
        pltpu.VMEM((count // 2 * channels, span), f32)
    ] * 2


def convolve_first(values, channels, span):
    count = values.shape[0]
    return pl.pallas_call(
        functools.partial(first_body, channels),
        out_shape=[shape_of((count, channels, span)), shape_of((1, count * span), f32)],
        in_specs=[VMEM],
        out_specs=[VMEM] * 2,
        scratch_shapes=scratch_for(count, channels, span),
        compiler_params=SMALL,
        cost_estimate=cost(1e6, 1e5),
        name="conv_first",
    )(values)


def rest_body(lag_row, *refs):
    chips = len(refs) - 10
    messages, keep, other = refs[:chips], refs[chips], refs[chips + 1]
    gathered, done, *scratch = refs[chips + 2 :]
    plus, minus = scratch[:2]
    chip, core = place()
    copies = []
    for slot, message in zip(leaving_order(chips), messages):
        base = 2 * jnp.bitwise_xor(chip, slot)
        copies.append(pltpu.make_async_copy(message, gathered.at[pl.ds(base, 2)], done.at[slot]))
        copies[-1].start()
    fill_strips(lag_row[...], plus, minus)
    for copy in copies:
        copy.wait()
    convolve(lambda at: gathered[at], *scratch)
    acc_plus, acc_minus = scratch[4:]
    count, channels, span = gathered.shape
    half = count // 2
    gathered[:half] = (acc_plus[...] + acc_minus[...]).reshape(half, channels, span).astype(bf16)
    gathered[half:] = (acc_plus[...] - acc_minus[...]).reshape(half, channels, span).astype(bf16)
    for slot in range(chips):
        base = 2 * jnp.bitwise_xor(chip, slot)
        keep[slot] = gathered[base + core]
        other[slot] = gathered[base + 1 - core]


def convolve_rest(lag_row, messages):
    chips = len(messages)
    _, channels, span = messages[0].shape
    result = shape_of((chips, channels, span))
    return pl.pallas_call(
        rest_body,
        out_shape=[result] * 2,
        in_specs=[VMEM] + [HBM] * chips,
        out_specs=[VMEM] * 2,
        scratch_shapes=[pltpu.VMEM((2 * chips, channels, span), bf16), pltpu.SemaphoreType.DMA((chips,))]
        + scratch_for(2 * chips, channels, span),
        compiler_params=SMALL,
        cost_estimate=cost(6e10, 1e8),
        name="conv_rest",
    )(lag_row, *messages)


def join_body(keep, other, *messages):
    for slot, message in enumerate(messages):
        message[0] = keep[slot]
        message[1] = other[slot]


def join(keep, other):
    chips, channels, span = keep.shape
    return pl.pallas_call(
        join_body,
        out_shape=[shape_of((2, channels, span))] * chips,
        in_specs=[VMEM] * 2,
        out_specs=[VMEM] * chips,
        compiler_params=SMALL,
        name="join",
    )(keep, other)


def mix_first_body(tokens, gate_weight, conv, weight, out, *late):
    devices, first, rows = conv.shape
    width, columns = weight.shape
    per = width // devices
    gate = jnp.dot(tokens[...], gate_weight[...], preferred_element_type=f32)
    silu = (gate / (1.0 + jnp.exp(-gate))).T
    used = weight[...]
    if late:
        silu = silu.reshape(devices // 4, 4 * per, rows)
        used = used.reshape(devices // 4, 4 * per, columns)
        late[0][...] = silu[:, 4 * first :].reshape(late[0].shape)
        late[1][...] = used[:, 4 * first :].reshape(late[1].shape)
        silu = silu[:, : 4 * first]
        used = used[:, : 4 * first].reshape(devices * first, columns)
    gated = (conv[...].astype(f32) * silu.reshape(devices, first, rows)).astype(bf16)
    mixed = jnp.dot(gated.reshape(devices * first, rows).T, used, preferred_element_type=f32)
    out[...] = mixed.astype(out.dtype)


def mix_first(tokens, gate_weight, conv, weight):
    devices, first, rows = conv.shape
    width, columns = weight.shape
    rest = width // devices - first
    outs = [shape_of((rows, columns), f32 if rest else bf16)]
    if rest:
        outs += [shape_of((devices, rest, rows), f32), shape_of((devices, rest, columns))]
    return pl.pallas_call(
        mix_first_body,
        out_shape=outs,
        in_specs=[VMEM] * 4,
        out_specs=[VMEM] * len(outs),
        compiler_params=SMALL,
        cost_estimate=cost(4 * width * rows * columns, 8 * rows * columns),
        name="mix_first",
    )(tokens, gate_weight, conv, weight)


def mix_rest_body(partial, silu, weight, *refs):
    messages, out = refs[:-4], refs[-4]
    gathered, out_here, out_done = refs[-3:]
    devices, rest, rows = gathered.shape
    chip, core = place()
    for slot, message in enumerate(messages):
        base = 2 * jnp.bitwise_xor(chip, slot)
        gathered[base + core] = message[0]
        gathered[base + 1 - core] = message[1]
    used = weight[...].reshape(devices * rest, weight.shape[2])
    writing = []
    for at in range(out_done.shape[0]):
        height = rows // out_done.shape[0]
        here = slice(height * at, height * at + height)
        gated = (gathered[:, :, here].astype(f32) * silu[:, :, here]).astype(bf16)
        gated = gated.reshape(devices * rest, height).T
        total = partial[here] + jnp.dot(gated, used, preferred_element_type=f32)
        out_here[here] = total.astype(bf16)
        writing.append(pltpu.make_async_copy(out_here.at[here], out.at[here], out_done.at[at]))
        writing[-1].start()
    for copy in writing:
        copy.wait()


def mix_rest(partial, silu, weight, messages):
    devices, rest, rows = silu.shape
    return pl.pallas_call(
        mix_rest_body,
        out_shape=shape_of(partial.shape),
        in_specs=[VMEM] * (3 + len(messages)),
        out_specs=HBM,
        scratch_shapes=[
            pltpu.VMEM((devices, rest, rows), bf16),
            pltpu.VMEM(partial.shape, bf16),
            pltpu.SemaphoreType.DMA((4,)),
        ],
        compiler_params=SMALL,
        cost_estimate=cost(2 * devices * rest * rows * weight.shape[2], 8 * rows * weight.shape[2]),
        name="mix_rest",
    )(partial, silu, weight, *messages)


def to_core(block, devices):
    return lax.ppermute(block, "seq", [(i, i ^ 1) for i in range(devices)])


def leaving_order(chips):
    half = chips // 2
    far = sorted(range(half, chips), key=lambda slot: (slot % 2 == 0, slot))
    return [0] + list(range(half - 1, 0, -1)) + far


def to_chips(messages, devices):
    got = [messages[0]]
    for slot in range(1, len(messages)):
        got.append(lax.ppermute(messages[slot], "seq", [(i, i ^ (2 * slot)) for i in range(devices)]))
    return got


def body(tokens, value_weight, gate_weight, out_weight, kernel_weight, kernel_bias):
    rows, width = tokens.shape
    devices = lax.axis_size("seq")
    per = width // devices
    heads = kernel_weight.shape[1]
    splits = per % (2 * TILE) == 0 and devices & (devices - 1) == 0 and devices % 4 == 0
    splits = splits and heads == devices and 2 * per % LANES == 0
    if splits:
        first = per // 2
        span = 4 * per
        cuts = [(span * at, span // 2) for at in range(devices // 4)]
        later = [(start + size, size) for start, size in cuts]
        pairs = [(at // 4 * 4 + at % 4 // 2, at // 4 * 4 + 2 + at % 4 // 2) for at in range(devices)]
        blocks = first_project(
            tokens, value_weight, kernel_weight, kernel_bias, devices, first, cuts, pairs
        )
    else:
        first = per
        alone = [(at * heads // devices,) for at in range(devices)]
        blocks = first_project(
            tokens, value_weight, kernel_weight, kernel_bias, devices, first, [(0, width)], alone
        )
    columns = lax.all_to_all(blocks, "seq", split_axis=0, concat_axis=0, tiled=True)
    if splits:
        keep, other = rest_project(tokens, value_weight, devices // 2, per - first, later)
        messages = to_chips(meet(keep, to_core(other, devices)), devices)
    convolved, lag_row = convolve_first(columns, first, rows)
    returned = lax.all_to_all(convolved, "seq", split_axis=0, concat_axis=0, tiled=True)
    if not splits:
        return mix_first(tokens, gate_weight, returned, out_weight)[0]
    messages = [messages[slot] for slot in leaving_order(devices // 2)]
    keep, other = convolve_rest(lag_row, messages)
    messages = to_chips(join(keep, to_core(other, devices)), devices)
    return mix_rest(*mix_first(tokens, gate_weight, returned, out_weight), messages)


def solution(mesh):
    placed = (P(("grp", "seq"), None), P(), P(), P(), P(), P())
    return jax.shard_map(
        body, mesh=mesh, in_specs=placed, out_specs=P(("grp", "seq"), None), check_vma=False
    )
```
